256 devices in a mesh: dp: 64 (over y_hi, z, x), tensor: 4 (over y_lo, core).
Axes of the slice: x: 4, y: 4 (y_hi: 2, y_lo: 2; y = y_hi * 2 + y_lo), z: 8, core: 2. Of those that a mesh axis runs over, the one named last changes fastest.
Arguments:
- activations: bfloat16 [16384, 8192], P('dp'), may hold values from -6 to 6
- out_grad: bfloat16 [16384, 22016], P('dp', 'tensor'), may hold values from -0.1875 to 0.1875
- basis: bfloat16 [8192, 512], P('dp', 'tensor'), may hold values from -0.0625 to 0.0625
- master: float32 [8192, 22016], P('dp', 'tensor'), may hold values from -4 to 4
- first_moment: float32 [512, 22016], P('dp', 'tensor'), may hold values from -6 to 6
- second_moment: float32 [512, 22016], P('dp', 'tensor'), may hold values from 0.01 to 0.25
Outputs:
- new_master: float32 [8192, 22016], P('dp', 'tensor')
- new_first: float32 [512, 22016], P('dp', 'tensor')
- new_second: float32 [512, 22016], P('dp', 'tensor')
The draws below stay inside these ranges and needn't reach their ends.
All inputs are finite; a program needn't handle non-finite values.
Results may differ from the reference program's by a relative error of at most 0.00059.
Values may be sent and summed in bfloat16 or wider, within the bound.
A program may use at most 128 MiB of HBM per device.

```python
import math
import jax
import jax.numpy as jnp
from jax import lax

D = 8192
FF = 22016
R = 512
TOKENS = 16384


def level_of(stream_key, shape, cuts, least, high):
    def one(position, blocks):
        steps = jax.random.uniform(jax.random.fold_in(jax.random.fold_in(stream_key, 6), position), (blocks,), jnp.float32, least / len(cuts), high / len(cuts))
        return jnp.repeat(jnp.exp(steps), shape[position] // blocks).reshape((-1,) + (1,) * (len(shape) - position - 1))

    factor_of = one(*cuts[0])
    for cut in cuts[1:]:
        factor_of = factor_of * one(*cut)
    return factor_of


def normal_values(own_key, dims, scale, reach, shards=(), held_as=jnp.bfloat16):
    result = jax.random.normal(own_key, dims, jnp.float32) * scale
    if len(shards) > 0:
        result = level_of(own_key, dims, shards, -0.22, 0.18) * result
    return jnp.clip(result, min=-reach, max=reach).astype(held_as)


def setup_inputs(seed: int = 0) -> dict:
    keys = jax.random.split(jax.random.key(seed), 7)
    return {
        "activations": normal_values(keys[0], (TOKENS, D), 1.0, 6.0, ((0, 64),)),
        "out_grad": normal_values(keys[1], (TOKENS, FF), (1.5 * TOKENS ** -0.5), 0.1875, ((0, 64), (1, 4))),
        "basis": normal_values(keys[2], (D, R), D ** -0.5, 0.0625, ((0, 64), (1, 4))),
        "master": normal_values(keys[3], (D, FF), 0.5, 4.0, ((0, 64), (1, 4)), jnp.float32),
        "first_moment": normal_values(keys[4], (R, FF), 1.0, 6.0, ((0, 64), (1, 4)), jnp.float32),
        "second_moment": jnp.clip(jnp.exp(math.log(0.25) - 3.218876 * jax.random.uniform(keys[5], (R, FF), jnp.float32) ** level_of(keys[5], (R, FF), ((0, 64), (1, 4)), -0.2, 0.2)), 0.01, 0.25),
    }


decay_first = 0.9
decay_second = 0.999
bias_first = 1.0 - math.exp(1000.0 * math.log(decay_first))
bias_second = 1.0 - math.exp(1000.0 * math.log(decay_second))
adam_eps = 1e-08
step_size = 0.025

def reference(activations, out_grad, basis, master, first_moment, second_moment):
    projected = jnp.dot(activations, basis, preferred_element_type=jnp.float32).astype(jnp.bfloat16)
    low_grad = lax.dot_general(projected, out_grad, (((0,), (0,)), ((), ())), preferred_element_type=jnp.float32)
    new_first = decay_first * first_moment + (1.0 - decay_first) * low_grad
    new_second = decay_second * second_moment + (1.0 - decay_second) * low_grad * low_grad
    factor = (new_first / bias_first / (jnp.sqrt(new_second / bias_second) + adam_eps)).astype(jnp.bfloat16)
    expanded = jnp.dot(basis, factor, preferred_element_type=jnp.float32)
    new_master = master - step_size * expanded
    return (new_master, new_first, new_second)
```

```python
import math

import jax
import jax.numpy as jnp
from jax import lax
from jax.experimental import pallas as pl
from jax.experimental.pallas import tpu as pltpu
from jax.sharding import PartitionSpec as P

MESH = pl.DeviceIdType.MESH
F32 = jnp.float32
BF16 = jnp.bfloat16

decay_first = 0.9
decay_second = 0.999
bias_first = 1.0 - math.exp(1000.0 * math.log(decay_first))
bias_second = 1.0 - math.exp(1000.0 * math.log(decay_second))
adam_eps = 1e-08
step_size = 0.025

NX, NZ, NG = 4, 8, 8
W = 768
TOP = 5504 // 128 - W // 128
CW = 384
NC = W // CW


def kernel(
    act_h, og_h, bas_h, mas_h, fm_h, sm_h,
    om, of, os_,
    act, og, bas, mas, projt, part, rsr, mom, sec, nfr, nsr, fac, lhs, exs, exr,
    lsem, bs, br, zs, zr, gs, gr, ms, mr, ps, pr, ys, yr, cs, cr,
    ts, tr, rs, rr, fs, fr, es, er, ns, nr,
):
    d = lax.axis_index("dp")
    t = lax.axis_index("tensor")
    x = lax.rem(d, 4)
    z = lax.rem(d // 4, 8)
    yh = d // 32
    g = yh * 4 + x

    def dev(yy, zz, xx):
        return yy * 32 + zz * 4 + xx

    def wrapz(v):
        return lax.rem(v + 16, 8)

    def member(j, sign):
        yy = lax.rem(yh + j // 4, 2)
        xx = lax.rem(x + sign * (j % 4) + 4, 4)
        return yy, xx

    def start_of(k):
        return pl.multiple_of(jnp.minimum(k * (W // 128), TOP) * 128, 128)

    def rcopy(src, dst, s, r, to):
        return pltpu.make_async_remote_copy(
            src_ref=src, dst_ref=dst, send_sem=s, recv_sem=r, device_id=to, device_id_type=MESH
        )

    t1 = t + 1 - 2 * lax.rem(t, 2)
    t2 = lax.rem(t + 2, 4)
    t3 = lax.rem(t1 + 2, 4)
    up, down = (dev(yh, wrapz(z + 1), x), t), (dev(yh, wrapz(z - 1), x), t)
    dy = dev(1 - yh, z, x)
    group = []
    for j in range(1, NG):
        yy, xx = member(j, 1)
        group.append((dev(yy, z, xx), t))
    partners = group + [up, down, (d, t1), (d, t2), (d, t3), (dy, t2)]

    loads = [
        pltpu.make_async_copy(act_h, act, lsem.at[0]),
        pltpu.make_async_copy(mas_h, mas, lsem.at[1]),
        pltpu.make_async_copy(og_h.at[:, pl.ds(start_of(g), W)], og.at[g], lsem.at[2]),
        pltpu.make_async_copy(bas_h, bas.at[z, g], lsem.at[3]),
        pltpu.make_async_copy(
            fm_h.at[:, pl.ds(start_of(g), W)], mom.at[pl.ds(pl.multiple_of(g * 8, 8), 8)], lsem.at[4]
        ),
        pltpu.make_async_copy(
            sm_h.at[:, pl.ds(start_of(g), W)], sec.at[pl.ds(pl.multiple_of(g * 8, 8), 8)], lsem.at[5]
        ),
    ]
    for c in loads:
        c.start()

    barrier = pltpu.get_barrier_semaphore()
    for p in partners:
        pl.semaphore_signal(barrier, inc=1, device_id=p, device_id_type=MESH)
    pl.semaphore_wait(barrier, len(partners))

    sends = []

    def go(c):
        c.start()
        sends.append(c)
        return c

    b_in = [go(rcopy(bas_h, bas.at[z, g], bs.at[j], br.at[j], group[j - 1])) for j in range(1, NG)]
    m_in, g_in = [], []
    for j in range(1, NG):
        yy, xx = member(j, 1)
        k = yy * 4 + xx
        rows = pl.ds(pl.multiple_of(g * 8, 8), 8)
        to = group[j - 1]
        g_in.append(go(rcopy(og_h.at[:, pl.ds(start_of(k), W)], og.at[g], gs.at[j], gr.at[j], to)))
    for j in range(1, NG):
        yy, xx = member(j, 1)
        k = yy * 4 + xx
        rows = pl.ds(pl.multiple_of(g * 8, 8), 8)
        to = group[j - 1]
        m_in.append(go(rcopy(fm_h.at[:, pl.ds(start_of(k), W)], mom.at[rows], ms.at[0, j], mr.at[0, j], to)))
        m_in.append(go(rcopy(sm_h.at[:, pl.ds(start_of(k), W)], sec.at[rows], ms.at[1, j], mr.at[1, j], to)))
    for c in b_in:
        c.wait_recv()
    loads[3].wait()

    def zsend(way, s, h):
        zz = wrapz(z - s) if way == 0 else wrapz(z + s)
        blk = bas.at[zz, pl.ds(h * 4, 4)]
        return go(rcopy(blk, blk, zs.at[way, s, h], zr.at[way, s, h], up if way == 0 else down))

    def hops(s):
        return [(w, h) for h in (0, 1) for w in (0, 1) if s < 3 or w == h]

    def project(zz, h):
        cols = pl.ds(pl.multiple_of((h * 32 + zz * 4) * 128, 512), 512)
        return jnp.dot(
            act[:, cols], bas[zz, h * 4 : h * 4 + 4].reshape(512, 128), preferred_element_type=F32
        )

    moving = {(0, w, h): zsend(w, 0, h) for w, h in hops(0)}
    t_in = []
    own = pl.ds(pl.multiple_of(t * 128, 128), 128)
    for i, q in enumerate((t1, t2, t3)):
        t_in.append(go(rcopy(bas.at[z], lhs.at[:, :, own], ts.at[i], tr.at[i], (d, q))))
    lhs[:, :, own] = bas[z]
    loads[0].wait()
    total = project(z, 0) + project(z, 1)
    for s in range(4):
        for w, h in hops(s):
            moving[(s, w, h)].wait_recv()
            if s < 3 and (w, h) in hops(s + 1):
                moving[(s + 1, w, h)] = zsend(w, s + 1, h)
        for w, h in hops(s):
            total = total + project(wrapz(z - s - 1) if w == 0 else wrapz(z + s + 1), h)

    rows_t = pl.ds(pl.multiple_of(t * 128, 128), 128)
    rows_u = pl.ds(pl.multiple_of(t2 * 128, 128), 128)
    cols_g = pl.ds(pl.multiple_of(g * 256, 256), 256)
    projt[rows_t, cols_g] = total.T.astype(BF16)
    p_in = []
    for j in range(1, NX):
        blk = projt.at[rows_t, cols_g]
        p_in.append(go(rcopy(blk, blk, ps.at[j], pr.at[j], group[j - 1])))
    for c in p_in:
        c.wait_recv()
    half = lambda yy: pl.ds(pl.multiple_of(yy * 1024, 1024), 1024)
    blk = projt.at[rows_t, half(yh)]
    y_in = [
        go(rcopy(blk, blk, ys.at[i], yr.at[i], to)) for i, to in enumerate([(d, t2), (dy, t2), (dy, t)])
    ]
    c_in = [go(rcopy(blk, blk, cs.at[3], cr.at[3], (d, t1)))]
    for i, (rows, yy) in enumerate([(rows_u, yh), (rows_u, 1 - yh), (rows_t, 1 - yh)]):
        y_in[i].wait_recv()
        blk = projt.at[rows, half(yy)]
        c_in.append(go(rcopy(blk, blk, cs.at[i], cr.at[i], (d, t1))))
    loads[2].wait()
    for c in g_in:
        c.wait_recv()
    for c in c_in:
        c.wait_recv()

    def multiply(i, carry):
        cols = pl.ds(pl.multiple_of(i * 256, 256), 256)
        part[:, cols] = jnp.dot(
            projt[...], og[:, :, cols].reshape(2048, 256), preferred_element_type=F32
        )
        return carry

    lax.fori_loop(0, W // 256, multiply, 0)

    def rows_of(w, b):
        return pl.ds(pl.multiple_of(w * 256 + b * 32, 32), 32)

    def rsend(w, c, s):
        b = wrapz(z - 1 - s) if w == 0 else wrapz(z + 1 + s)
        src = part.at[rows_of(w, b), pl.ds(c * CW, CW)]
        return go(rcopy(src, rsr.at[w, c, s], rs.at[w, c, s], rr.at[w, c, s], up if w == 0 else down))

    moving = {(w, c): rsend(w, c, 0) for c in range(NC) for w in (0, 1)}
    for s in range(7):
        for c in range(NC):
            for w in (0, 1):
                moving[(w, c)].wait_recv()
                b = wrapz(z - 2 - s) if w == 0 else wrapz(z + 2 + s)
                cols = pl.ds(c * CW, CW)
                part[rows_of(w, b), cols] = part[rows_of(w, b), cols] + rsr[w, c, s]
                if s < 6:
                    moving[(w, c)] = rsend(w, c, s + 1)

    loads[4].wait()
    loads[5].wait()
    for c in m_in:
        c.wait_recv()
    for w in (0, 1):
        rows = slice(w * 32, w * 32 + 32)
        grad = part[rows_of(w, z), :]
        first = decay_first * mom[rows] + (1.0 - decay_first) * grad
        second = decay_second * sec[rows] + (1.0 - decay_second) * grad * grad
        mom[rows] = first
        sec[rows] = second
        fac[w, z] = (
            first / bias_first / (jnp.sqrt(second / bias_second) + adam_eps)
        ).astype(BF16)

    def fsend(way, s, h):
        zz = wrapz(z - s) if way == 0 else wrapz(z + s)
        blk = fac.at[h, zz]
        return go(rcopy(blk, blk, fs.at[way, s, h], fr.at[way, s, h], up if way == 0 else down))

    moving = {(0, w, h): fsend(w, 0, h) for w, h in hops(0)}
    n_in = []
    for j in range(1, NG):
        yy, xx = member(j, 1)
        k = yy * 4 + xx
        rows = pl.ds(pl.multiple_of(k * 8, 8), 8)
        to = group[j - 1]
        n_in.append(go(rcopy(mom.at[rows], nfr.at[g], ns.at[0, j], nr.at[0, j], to)))
        n_in.append(go(rcopy(sec.at[rows], nsr.at[g], ns.at[1, j], nr.at[1, j], to)))
    mine = pl.ds(pl.multiple_of(g * 8, 8), 8)
    nfr[g] = mom[mine]
    nsr[g] = sec[mine]
    for s in range(4):
        for w, h in hops(s):
            moving[(s, w, h)].wait_recv()
            if s < 3 and (w, h) in hops(s + 1):
                moving[(s + 1, w, h)] = fsend(w, s + 1, h)

    for c in t_in:
        c.wait_recv()
    e_in = []
    for j in (6, 2, 5, 7, 4, 1, 3, 0):
        yy, xx = member(j, 1)
        k = yy * 4 + xx
        res = jnp.dot(lhs[k], fac[...].reshape(512, W), preferred_element_type=F32)
        if j == 0:
            exr[g] = res
        else:
            exs[j] = res
            e_in.append((j, go(rcopy(exs.at[j], exr.at[g], es.at[j], er.at[j], group[j - 1]))))

    for c in n_in:
        c.wait_recv()
    loads[1].wait()
    for k in range(NG):
        at = min(k * (W // 128), TOP) * 128
        of[:, at : at + W] = nfr[k]
        os_[:, at : at + W] = nsr[k]

    def finish(k):
        cols = pl.ds(start_of(k), W)
        om[:, cols] = mas[:, cols] - step_size * exr[k]

    finish(g)
    for j, c in e_in:
        c.wait_recv()
        yy, xx = member(j, -1)
        finish(yy * 4 + xx)
    for c in sends:
        c.wait_send()


def local(activations, out_grad, basis, master, first_moment, second_moment):
    dma = pltpu.SemaphoreType.DMA
    sems = [
        dma((6,)),
        dma((8,)), dma((8,)),
        dma((2, 4, 2)), dma((2, 4, 2)),
        dma((8,)), dma((8,)),
        dma((2, 8)), dma((2, 8)),
        dma((4,)), dma((4,)),
        dma((3,)), dma((3,)),
        dma((4,)), dma((4,)),
        dma((3,)), dma((3,)),
        dma((2, NC, 7)), dma((2, NC, 7)),
        dma((2, 4, 2)), dma((2, 4, 2)),
        dma((8,)), dma((8,)),
        dma((2, 8)), dma((2, 8)),
    ]
    return pl.pallas_call(
        kernel,
        out_shape=(
            jax.ShapeDtypeStruct((128, 5504), F32),
            jax.ShapeDtypeStruct((8, 5504), F32),
            jax.ShapeDtypeStruct((8, 5504), F32),
        ),
        in_specs=[pl.BlockSpec(memory_space=pl.ANY)] * 6,
        out_specs=[pl.BlockSpec(memory_space=pltpu.VMEM)] * 3,
        scratch_shapes=[
            pltpu.VMEM((256, 8192), BF16),
            pltpu.VMEM((NG, 256, W), BF16),
            pltpu.VMEM((NZ, NG, 128, 128), BF16),
            pltpu.VMEM((128, 5504), F32),
            pltpu.VMEM((512, 2048), BF16),
            pltpu.VMEM((512, W), F32),
            pltpu.VMEM((2, NC, 7, 32, CW), F32),
            pltpu.VMEM((64, W), F32),
            pltpu.VMEM((64, W), F32),
            pltpu.VMEM((NG, 8, W), F32),
            pltpu.VMEM((NG, 8, W), F32),
            pltpu.VMEM((2, NZ, 32, W), BF16),
            pltpu.VMEM((NG, 128, 512), BF16),
            pltpu.VMEM((NG, 128, W), F32),
            pltpu.VMEM((NG, 128, W), F32),
        ]
        + sems,
        compiler_params=pltpu.CompilerParams(
            collective_id=0, has_side_effects=True, vmem_limit_bytes=56 << 20
        ),
    )(activations, out_grad, basis, master, first_moment, second_moment)


def solution(mesh):
    placed = (
        P("dp", None),
        P("dp", "tensor"),
        P("dp", "tensor"),
        P("dp", "tensor"),
        P("dp", "tensor"),
        P("dp", "tensor"),
    )
    return jax.shard_map(
        local,
        mesh=mesh,
        in_specs=placed,
        out_specs=(P("dp", "tensor"), P("dp", "tensor"), P("dp", "tensor")),
        check_vma=False,
    )
```

```python
import math

import jax
import jax.numpy as jnp
from jax import lax
from jax.experimental import pallas as pl
from jax.experimental.pallas import tpu as pltpu
from jax.sharding import PartitionSpec as P

MESH = pl.DeviceIdType.MESH
F32 = jnp.float32
BF16 = jnp.bfloat16

decay_first = 0.9
decay_second = 0.999
bias_first = 1.0 - math.exp(1000.0 * math.log(decay_first))
bias_second = 1.0 - math.exp(1000.0 * math.log(decay_second))
adam_eps = 1e-08
step_size = 0.025

NX, NZ, NG = 4, 8, 8
W = 768
TOP = 5504 // 128 - W // 128
CW = 256
NC = W // CW
ORDER = (6, 2, 5, 7, 4, 1, 3)


def kernel(
    act_h, og_h, bas_h, mas_h, fm_h, sm_h,
    om, of, os_,
    act, og, bas, mas, projt, part, rsr, mom, sec, nfr, nsr, fac, home, lhs, exs, exr,
    lsem, bs, br, zs, zr, gs, gr, ms, mr, p1s, p1r, p2s, p2r, cs, cr,
    ts, tr, rs, rr, fs, fr, qs, qr, us, ur, es, er, ns, nr,
):
    d = lax.axis_index("dp")
    t = lax.axis_index("tensor")
    x = lax.rem(d, 4)
    z = lax.rem(d // 4, 8)
    yh = d // 32
    g = yh * 4 + x

    def dev(yy, zz, xx):
        return yy * 32 + zz * 4 + xx

    def wrapz(v):
        return lax.rem(v + 16, 8)

    def member(j, sign):
        yy = lax.rem(yh + j // 4, 2)
        xx = lax.rem(x + sign * (j % 4) + 4, 4)
        return yy, xx

    def index(j, sign):
        yy, xx = member(j, sign)
        return yy * 4 + xx

    def start_of(k):
        return pl.multiple_of(jnp.minimum(k * (W // 128), TOP) * 128, 128)

    def span(first, size):
        return pl.ds(pl.multiple_of(first, size), size)

    def rcopy(src, dst, s, r, to):
        return pltpu.make_async_remote_copy(
            src_ref=src, dst_ref=dst, send_sem=s, recv_sem=r, device_id=to, device_id_type=MESH
        )

    t1 = t + 1 - 2 * lax.rem(t, 2)
    t2 = lax.rem(t + 2, 4)
    ring = ((dev(yh, wrapz(z + 1), x), t), (dev(yh, wrapz(z - 1), x), t))
    dy = dev(1 - yh, z, x)
    group = [None]
    for j in range(1, NG):
        yy, xx = member(j, 1)
        group.append((dev(yy, z, xx), t))
    core = (d, t1)
    yside = ((d, t2), (dy, t2), (dy, t))
    partners = group[1:] + [ring[0], ring[1], core, (d, t2), (dy, t2)]

    eight = span(g * 8, 8)
    loads = [
        pltpu.make_async_copy(bas_h, bas.at[z, g], lsem.at[3]),
        pltpu.make_async_copy(act_h, act, lsem.at[0]),
        pltpu.make_async_copy(mas_h, mas, lsem.at[1]),
        pltpu.make_async_copy(og_h.at[:, pl.ds(start_of(g), W)], og.at[g], lsem.at[2]),
        pltpu.make_async_copy(fm_h.at[:, pl.ds(start_of(g), W)], mom.at[eight], lsem.at[4]),
        pltpu.make_async_copy(sm_h.at[:, pl.ds(start_of(g), W)], sec.at[eight], lsem.at[5]),
    ]
    for c in loads:
        c.start()

    barrier = pltpu.get_barrier_semaphore()
    for p in partners:
        pl.semaphore_signal(barrier, inc=1, device_id=p, device_id_type=MESH)
    pl.semaphore_wait(barrier, len(partners))

    sends = []

    def go(c):
        c.start()
        sends.append(c)
        return c

    b_in = [go(rcopy(bas_h, bas.at[z, g], bs.at[j], br.at[j], group[j])) for j in ORDER]
    for c in b_in:
        c.wait_recv()
    loads[0].wait()

    def hops(s):
        return [(w, h) for h in (0, 1) for w in (0, 1) if s < 3 or w == h]

    def gather(block, send, recv):
        moving = {}

        def send_step(s):
            for w, h in hops(s):
                if s > 0:
                    moving[(s - 1, w, h)].wait_recv()
                zz = wrapz(z - s) if w == 0 else wrapz(z + s)
                blk = block(zz, h)
                moving[(s, w, h)] = go(rcopy(blk, blk, send.at[w, s, h], recv.at[w, s, h], ring[w]))

        def last():
            for s in (2, 3):
                for w, h in hops(s):
                    if (s, w, h) in moving and not (s == 2 and (w, h) in hops(3)):
                        moving[(s, w, h)].wait_recv()

        return send_step, last

    def project(zz, h):
        return jnp.dot(
            act[:, span((h * 32 + zz * 4) * 128, 512)],
            bas[zz, h * 4 : h * 4 + 4].reshape(512, 128),
            preferred_element_type=F32,
        )

    step, last = gather(lambda zz, h: bas.at[zz, pl.ds(h * 4, 4)], zs, zr)
    step(0)

    def grad_send(i, first, size):
        return [
            go(
                rcopy(
                    og_h.at[:, pl.ds(pl.multiple_of(start_of(index(j, 1)) + first, 128), size)],
                    og.at[g, :, pl.ds(first, size)],
                    gs.at[i, j],
                    gr.at[i, j],
                    group[j],
                )
            )
            for j in ORDER
        ]

    g_in = [grad_send(0, 0, 512)]
    rows_t, rows_u = span(t * 128, 128), span(t2 * 128, 128)
    t_in = [go(rcopy(bas.at[z], lhs.at[:, :, rows_t], ts.at[0], tr.at[0], core))]
    lhs[:, :, rows_t] = bas[z]
    loads[1].wait()
    total = project(z, 0) + project(z, 1)
    for s in range(1, 4):
        step(s)
        for w, h in hops(s - 1):
            if s < 3 or (w, h) in hops(3):
                total = total + project(wrapz(z - s) if w == 0 else wrapz(z + s), h)
    last()
    for w, h in hops(2):
        if (w, h) not in hops(3):
            total = total + project(wrapz(z - 3) if w == 0 else wrapz(z + 3), h)
    for w, h in hops(3):
        total = total + project(wrapz(z - 4), h)

    top_t, low_t = span(t * 128, 64), pl.ds(pl.multiple_of(t * 128 + 64, 64), 64)
    top_u, low_u = span(t2 * 128, 64), pl.ds(pl.multiple_of(t2 * 128 + 64, 64), 64)
    cols_x = span(x * 256, 256)
    projt[yh, rows_t, cols_x] = total.T.astype(BF16)
    blk = projt.at[yh, top_t, cols_x]
    xa = [go(rcopy(blk, blk, p1s.at[j], p1r.at[j], group[j])) for j in (2, 1, 3)]
    blk = projt.at[yh, low_t, cols_x]
    yb = [go(rcopy(blk, blk, p1s.at[4 + i], p1r.at[4 + i], to)) for i, to in enumerate(yside)]
    for c in xa:
        c.wait_recv()
    blk = projt.at[yh, top_t]
    ya = [go(rcopy(blk, blk, p2s.at[i], p2r.at[i], to)) for i, to in enumerate(yside)]
    for c in yb:
        c.wait_recv()
    xb = []
    for i, rows in enumerate((low_t, low_u)):
        blk = projt.at[:, rows, cols_x]
        xb += [go(rcopy(blk, blk, p2s.at[4 * i + 3 + j], p2r.at[4 * i + 3 + j], group[j])) for j in (2, 1, 3)]
    blk = projt.at[yh, top_t]
    c_in = [go(rcopy(blk, blk, cs.at[0], cr.at[0], core))]
    for i, (rows, yy) in enumerate([(top_u, yh), (top_u, 1 - yh), (top_t, 1 - yh)]):
        ya[i].wait_recv()
        blk = projt.at[yy, rows]
        c_in.append(go(rcopy(blk, blk, cs.at[i + 1], cr.at[i + 1], core)))
    for i, rows in enumerate((low_t, low_u)):
        for c in xb[3 * i : 3 * i + 3]:
            c.wait_recv()
        blk = projt.at[:, rows]
        c_in.append(go(rcopy(blk, blk, cs.at[i + 4], cr.at[i + 4], core)))
    for c in c_in:
        c.wait_recv()
    loads[3].wait()
    for c in g_in[0]:
        c.wait_recv()

    def multiply(c):
        cols = slice(c * CW, c * CW + CW)
        part[:, cols] = jnp.dot(
            projt[0], og[0:4, :, cols].reshape(1024, CW), preferred_element_type=F32
        ) + jnp.dot(projt[1], og[4:8, :, cols].reshape(1024, CW), preferred_element_type=F32)

    def rows_of(w, b):
        return pl.ds(pl.multiple_of(w * 256 + b * 32, 32), 32)

    def rsend(w, h, c, s):
        b = wrapz(z + 4 - s) if w == 0 else wrapz(z - 4 + s)
        src = part.at[rows_of(h, b), pl.ds(c * CW, CW)]
        return go(rcopy(src, rsr.at[w, h, c, s], rs.at[w, h, c, s], rr.at[w, h, c, s], ring[w]))

    moving = {}

    def begin(c):
        multiply(c)
        for w, h in ((0, 0), (1, 1), (0, 1), (1, 0)):
            moving[(w, h, c)] = rsend(w, h, c, 0 if w == h else 1)

    def reduce(c, s):
        for w, h in ((0, 0), (1, 1), (0, 1), (1, 0)):
            if s == 0 and w != h:
                continue
            moving[(w, h, c)].wait_recv()
            b = wrapz(z + 3 - s) if w == 0 else wrapz(z - 3 + s)
            cols = pl.ds(c * CW, CW)
            part[rows_of(h, b), cols] = part[rows_of(h, b), cols] + rsr[w, h, c, s]
            if s < 3:
                moving[(w, h, c)] = rsend(w, h, c, s + 1)

    def adam(c, put):
        cols = slice(c * CW, c * CW + CW)
        for w in (0, 1):
            rows = slice(w * 32, w * 32 + 32)
            grad = part[rows_of(w, z), cols]
            first = decay_first * mom[rows, cols] + (1.0 - decay_first) * grad
            second = decay_second * sec[rows, cols] + (1.0 - decay_second) * grad * grad
            mom[rows, cols] = first
            sec[rows, cols] = second
            put(w, (first / bias_first / (jnp.sqrt(second / bias_second) + adam_eps)).astype(BF16))

    def put_home(w, v):
        home[g, w, z] = v

    def put_fac(c):
        def put(w, v):
            fac[c - 1, w, z] = v

        return put

    begin(1)
    begin(0)
    m_in = []
    for j in ORDER:
        cols = pl.ds(start_of(index(j, 1)), W)
        m_in.append(go(rcopy(fm_h.at[:, cols], mom.at[eight], ms.at[0, j], mr.at[0, j], group[j])))
        m_in.append(go(rcopy(sm_h.at[:, cols], sec.at[eight], ms.at[1, j], mr.at[1, j], group[j])))
    g_in.append(grad_send(1, 512, 256))
    t_in.append(go(rcopy(bas.at[z], lhs.at[:, :, rows_t], ts.at[1], tr.at[1], (d, t2))))
    for s in range(4):
        reduce(1, s)
        reduce(0, s)
    loads[4].wait()
    loads[5].wait()
    for c in m_in:
        c.wait_recv()
    step1, last1 = gather(lambda zz, h: fac.at[0, h, zz], fs.at[0], fr.at[0])
    step2, last2 = gather(lambda zz, h: fac.at[1, h, zz], fs.at[1], fr.at[1])
    step0, last0 = gather(lambda zz, h: home.at[:, h, zz], us, ur)
    adam(1, put_fac(1))
    step1(0)
    adam(0, put_home)
    blk = home.at[g, :, z]
    q_in = [go(rcopy(blk, blk, qs.at[j], qr.at[j], group[j])) for j in ORDER]
    for c in g_in[1]:
        c.wait_recv()
    begin(2)
    step1(1)
    reduce(2, 0)
    step1(2)
    reduce(2, 1)
    step1(3)
    reduce(2, 2)
    t_in[1].wait_recv()
    blk = lhs.at[:, :, rows_u]
    t_in.append(go(rcopy(blk, blk, ts.at[2], tr.at[2], core)))
    last1()

    e_in = {}

    def expand(c):
        for j in ORDER + (0,):
            res = jnp.dot(lhs[index(j, 1)], fac[c - 1].reshape(512, CW), preferred_element_type=F32)
            cols = slice((c - 1) * CW, c * CW)
            if j == 0:
                exr[g, :, cols] = res
            else:
                exs[j, :, cols] = res
                e_in[(c, j)] = go(
                    rcopy(
                        exs.at[j, :, cols],
                        exr.at[g, :, cols],
                        es.at[c - 1, j],
                        er.at[c - 1, j],
                        group[j],
                    )
                )

    for c in t_in:
        if c is not t_in[1]:
            c.wait_recv()
    expand(1)
    reduce(2, 3)
    adam(2, put_fac(2))
    step2(0)
    for c in q_in:
        c.wait_recv()
    step0(0)
    n_in = []
    for j in ORDER:
        rows = span(index(j, 1) * 8, 8)
        n_in.append(go(rcopy(mom.at[rows], nfr.at[g], ns.at[0, j], nr.at[0, j], group[j])))
        n_in.append(go(rcopy(sec.at[rows], nsr.at[g], ns.at[1, j], nr.at[1, j], group[j])))
    nfr[g] = mom[eight]
    nsr[g] = sec[eight]
    step2(1)
    step2(2)
    step2(3)
    step0(1)
    last2()
    expand(2)
    for c in n_in:
        c.wait_recv()
    for k in range(NG):
        at = min(k * (W // 128), TOP) * 128
        of[:, at : at + W] = nfr[k]
        os_[:, at : at + W] = nsr[k]
    loads[2].wait()
    step0(2)
    step0(3)
    last0()
    for k in range(NG):
        at = min(k * (W // 128), TOP) * 128
        res = jnp.dot(lhs[g], home[k].reshape(512, CW), preferred_element_type=F32)
        om[:, at : at + CW] = mas[:, at : at + CW] - step_size * res

    def finish(k):
        cols = pl.ds(pl.multiple_of(start_of(k) + CW, 128), W - CW)
        om[:, cols] = mas[:, cols] - step_size * exr[k]

    finish(g)
    for j in ORDER:
        e_in[(1, j)].wait_recv()
        e_in[(2, j)].wait_recv()
        finish(index(j, -1))
    for c in sends:
        c.wait_send()


def local(activations, out_grad, basis, master, first_moment, second_moment):
    dma = pltpu.SemaphoreType.DMA
    sems = [dma((6,))]
    for shape in (
        (8,),
        (2, 4, 2),
        (2, 8),
        (2, 8),
        (8,),
        (12,),
        (6,),
        (3,),
        (2, 2, NC, 4),
        (2, 2, 4, 2),
        (8,),
        (2, 4, 2),
        (2, 8),
        (2, 8),
    ):
        sems += [dma(shape), dma(shape)]
    return pl.pallas_call(
        kernel,
        out_shape=(
            jax.ShapeDtypeStruct((128, 5504), F32),
            jax.ShapeDtypeStruct((8, 5504), F32),
            jax.ShapeDtypeStruct((8, 5504), F32),
        ),
        in_specs=[pl.BlockSpec(memory_space=pl.ANY)] * 6,
        out_specs=[pl.BlockSpec(memory_space=pltpu.VMEM)] * 3,
        scratch_shapes=[
            pltpu.VMEM((256, 8192), BF16),
            pltpu.VMEM((NG, 256, W), BF16),
            pltpu.VMEM((NZ, NG, 128, 128), BF16),
            pltpu.VMEM((128, 5504), F32),
            pltpu.VMEM((2, 512, 1024), BF16),
            pltpu.VMEM((512, W), F32),
            pltpu.VMEM((2, 2, NC, 4, 32, CW), F32),
            pltpu.VMEM((64, W), F32),
            pltpu.VMEM((64, W), F32),
            pltpu.VMEM((NG, 8, W), F32),
            pltpu.VMEM((NG, 8, W), F32),
            pltpu.VMEM((2, 2, NZ, 32, CW), BF16),
            pltpu.VMEM((NG, 2, NZ, 32, CW), BF16),
            pltpu.VMEM((NG, 128, 512), BF16),
            pltpu.VMEM((NG, 128, W - CW), F32),
            pltpu.VMEM((NG, 128, W - CW), F32),
        ]
        + sems,
        compiler_params=pltpu.CompilerParams(
            collective_id=0, has_side_effects=True, vmem_limit_bytes=56 << 20
        ),
    )(activations, out_grad, basis, master, first_moment, second_moment)


def solution(mesh):
    placed = (
        P("dp", None),
        P("dp", "tensor"),
        P("dp", "tensor"),
        P("dp", "tensor"),
        P("dp", "tensor"),
        P("dp", "tensor"),
    )
    return jax.shard_map(
        local,
        mesh=mesh,
        in_specs=placed,
        out_specs=(P("dp", "tensor"), P("dp", "tensor"), P("dp", "tensor")),
        check_vma=False,
    )
```

```python
import math

import jax
import jax.numpy as jnp
from jax import lax
from jax.experimental import pallas as pl
from jax.experimental.pallas import tpu as pltpu
from jax.sharding import PartitionSpec as P

MESH = pl.DeviceIdType.MESH
F32 = jnp.float32
BF16 = jnp.bfloat16

decay_first = 0.9
decay_second = 0.999
bias_first = 1.0 - math.exp(1000.0 * math.log(decay_first))
bias_second = 1.0 - math.exp(1000.0 * math.log(decay_second))
adam_eps = 1e-08
step_size = 0.025

NX, NZ, NG = 4, 8, 8
W = 768
TOP = 5504 // 128 - W // 128
CW = 256
NC = W // CW
ORDER = (6, 2, 5, 7, 4, 1, 3)


def kernel(
    act_h, og_h, bas_h, mas_h, fm_h, sm_h,
    om, of, os_,
    act, og, bas, mas, projt, part, ra, rb, rc, rd, mom, sec, nfr, nsr, fac, home, lhs, exs, exr,
    lsem, bs, br, zs, zr, gs, gr, ms, mr, p1s, p1r, p2s, p2r, cs, cr,
    ts, tr, rs, rr, fs, fr, qs, qr, us, ur, es, er, ns, nr,
):
    d = lax.axis_index("dp")
    t = lax.axis_index("tensor")
    x = lax.rem(d, 4)
    z = lax.rem(d // 4, 8)
    yh = d // 32
    g = yh * 4 + x

    def dev(yy, zz, xx):
        return yy * 32 + zz * 4 + xx

    def wrapz(v):
        return lax.rem(v + 16, 8)

    def member(j, sign):
        yy = lax.rem(yh + j // 4, 2)
        xx = lax.rem(x + sign * (j % 4) + 4, 4)
        return yy, xx

    def index(j, sign):
        yy, xx = member(j, sign)
        return yy * 4 + xx

    def start_of(k):
        return pl.multiple_of(jnp.minimum(k * (W // 128), TOP) * 128, 128)

    def span(first, size):
        return pl.ds(pl.multiple_of(first, size), size)

    def rcopy(src, dst, s, r, to):
        return pltpu.make_async_remote_copy(
            src_ref=src, dst_ref=dst, send_sem=s, recv_sem=r, device_id=to, device_id_type=MESH
        )

    t1 = t + 1 - 2 * lax.rem(t, 2)
    t2 = lax.rem(t + 2, 4)
    ring = ((dev(yh, wrapz(z + 1), x), t), (dev(yh, wrapz(z - 1), x), t))
    far = ((dev(yh, wrapz(z + 2), x), t), (dev(yh, wrapz(z - 2), x), t))
    dy = dev(1 - yh, z, x)
    group = [None]
    for j in range(1, NG):
        yy, xx = member(j, 1)
        group.append((dev(yy, z, xx), t))
    core = (d, t1)
    yside = ((d, t2), (dy, t2), (dy, t))
    partners = group[1:] + [ring[0], ring[1], far[0], far[1], core, (d, t2), (dy, t2)]

    eight = span(g * 8, 8)
    loads = [
        pltpu.make_async_copy(bas_h, bas.at[z, g], lsem.at[3]),
        pltpu.make_async_copy(act_h, act, lsem.at[0]),
        pltpu.make_async_copy(mas_h, mas, lsem.at[1]),
        pltpu.make_async_copy(og_h.at[:, pl.ds(start_of(g), W)], og.at[g], lsem.at[2]),
        pltpu.make_async_copy(fm_h.at[:, pl.ds(start_of(g), W)], mom.at[eight], lsem.at[4]),
        pltpu.make_async_copy(sm_h.at[:, pl.ds(start_of(g), W)], sec.at[eight], lsem.at[5]),
    ]
    for c in loads:
        c.start()

    barrier = pltpu.get_barrier_semaphore()
    for p in partners:
        pl.semaphore_signal(barrier, inc=1, device_id=p, device_id_type=MESH)
    pl.semaphore_wait(barrier, len(partners))

    sends = []

    def go(c):
        c.start()
        sends.append(c)
        return c

    b_in = [go(rcopy(bas_h, bas.at[z, g], bs.at[j], br.at[j], group[j])) for j in ORDER]
    for c in b_in:
        c.wait_recv()
    loads[0].wait()

    def hops(s):
        return [(w, h) for h in (0, 1) for w in (0, 1) if s < 3 or w == h]

    def gather(block, send, recv):
        moving = {}

        def send_step(s):
            for w, h in hops(s):
                if s > 0:
                    moving[(s - 1, w, h)].wait_recv()
                zz = wrapz(z - s) if w == 0 else wrapz(z + s)
                blk = block(zz, h)
                moving[(s, w, h)] = go(rcopy(blk, blk, send.at[w, s, h], recv.at[w, s, h], ring[w]))

        def last():
            for s in (2, 3):
                for w, h in hops(s):
                    if (s, w, h) in moving and not (s == 2 and (w, h) in hops(3)):
                        moving[(s, w, h)].wait_recv()

        return send_step, last

    def project(zz, h):
        return jnp.dot(
            act[:, span((h * 32 + zz * 4) * 128, 512)],
            bas[zz, h * 4 : h * 4 + 4].reshape(512, 128),
            preferred_element_type=F32,
        )

    step, last = gather(lambda zz, h: bas.at[zz, pl.ds(h * 4, 4)], zs, zr)
    step(0)

    def grad_send(i, first, size):
        return [
            go(
                rcopy(
                    og_h.at[:, pl.ds(pl.multiple_of(start_of(index(j, 1)) + first, 128), size)],
                    og.at[g, :, pl.ds(first, size)],
                    gs.at[i, j],
                    gr.at[i, j],
                    group[j],
                )
            )
            for j in ORDER
        ]

    g_in = [grad_send(0, 0, 512)]
    rows_t, rows_u = span(t * 128, 128), span(t2 * 128, 128)
    t_in = [go(rcopy(bas.at[z], lhs.at[:, :, rows_t], ts.at[0], tr.at[0], core))]
    lhs[:, :, rows_t] = bas[z]
    loads[1].wait()
    total = project(z, 0) + project(z, 1)
    for s in range(1, 4):
        step(s)
        for w, h in hops(s - 1):
            if s < 3 or (w, h) in hops(3):
                total = total + project(wrapz(z - s) if w == 0 else wrapz(z + s), h)
    last()
    for w, h in hops(2):
        if (w, h) not in hops(3):
            total = total + project(wrapz(z - 3) if w == 0 else wrapz(z + 3), h)
    for w, h in hops(3):
        total = total + project(wrapz(z - 4), h)

    top_t, low_t = span(t * 128, 64), pl.ds(pl.multiple_of(t * 128 + 64, 64), 64)
    top_u, low_u = span(t2 * 128, 64), pl.ds(pl.multiple_of(t2 * 128 + 64, 64), 64)
    cols_x = span(x * 256, 256)
    projt[yh, rows_t, cols_x] = total.T.astype(BF16)
    blk = projt.at[yh, top_t, cols_x]
    xa = [go(rcopy(blk, blk, p1s.at[j], p1r.at[j], group[j])) for j in (2, 1, 3)]
    blk = projt.at[yh, low_t, cols_x]
    yb = [go(rcopy(blk, blk, p1s.at[4 + i], p1r.at[4 + i], to)) for i, to in enumerate(yside)]
    for c in xa:
        c.wait_recv()
    blk = projt.at[yh, top_t]
    ya = [go(rcopy(blk, blk, p2s.at[i], p2r.at[i], to)) for i, to in enumerate(yside)]
    for c in yb:
        c.wait_recv()
    xb = []
    for i, rows in enumerate((low_t, low_u)):
        blk = projt.at[:, rows, cols_x]
        xb += [go(rcopy(blk, blk, p2s.at[4 * i + 3 + j], p2r.at[4 * i + 3 + j], group[j])) for j in (2, 1, 3)]
    m_in = []
    for j in ORDER:
        cols = pl.ds(start_of(index(j, 1)), W)
        m_in.append(go(rcopy(fm_h.at[:, cols], mom.at[eight], ms.at[0, j], mr.at[0, j], group[j])))
        m_in.append(go(rcopy(sm_h.at[:, cols], sec.at[eight], ms.at[1, j], mr.at[1, j], group[j])))
    blk = projt.at[yh, top_t]
    c_in = [go(rcopy(blk, blk, cs.at[0], cr.at[0], core))]
    for i, (rows, yy) in enumerate([(top_u, yh), (top_u, 1 - yh), (top_t, 1 - yh)]):
        ya[i].wait_recv()
        blk = projt.at[yy, rows]
        c_in.append(go(rcopy(blk, blk, cs.at[i + 1], cr.at[i + 1], core)))
    for i, rows in enumerate((low_t, low_u)):
        for c in xb[3 * i : 3 * i + 3]:
            c.wait_recv()
        blk = projt.at[:, rows]
        c_in.append(go(rcopy(blk, blk, cs.at[i + 4], cr.at[i + 4], core)))
    for c in c_in:
        c.wait_recv()
    loads[3].wait()
    for c in g_in[0]:
        c.wait_recv()

    def multiply(c):
        cols = slice(c * CW, c * CW + CW)
        total = jnp.dot(
            projt[0], og[0:4, :, cols].reshape(1024, CW), preferred_element_type=F32
        ) + jnp.dot(projt[1], og[4:8, :, cols].reshape(1024, CW), preferred_element_type=F32)
        part[:, :, cols] = total.reshape(2, 256, CW)

    def rank_rows(w, away):
        return span(wrapz(z + away if w == 0 else z - away) * 32, 32)

    hop = {}

    def leg(c, w, kind, src, dst, to):
        hop[(c, w, kind)] = go(rcopy(src, dst.at[c, w], rs.at[c, w, kind], rr.at[c, w, kind], to[w]))

    def begin(c):
        multiply(c)
        cols = pl.ds(c * CW, CW)
        for w in (0, 1):
            leg(c, w, 0, part.at[:, rank_rows(w, 3), cols], ra, ring)
            leg(c, w, 1, part.at[w, rank_rows(w, 4), cols], rb, far)
        for w in (0, 1):
            leg(c, w, 2, part.at[:, rank_rows(w, 1), cols], rc, ring)

    def middle(c):
        cols = pl.ds(c * CW, CW)
        for w in (0, 1):
            rows = rank_rows(w, 2)
            hop[(c, w, 0)].wait_recv()
            part[:, rows, cols] = part[:, rows, cols] + ra[c, w]
            hop[(c, w, 1)].wait_recv()
            part[w, rows, cols] = part[w, rows, cols] + rb[c, w]
            leg(c, w, 3, part.at[:, rows, cols], rd, far)

    def close(c):
        cols = pl.ds(c * CW, CW)
        rows = rank_rows(0, 0)
        for w in (0, 1):
            hop[(c, w, 2)].wait_recv()
            hop[(c, w, 3)].wait_recv()
            part[:, rows, cols] = part[:, rows, cols] + (rc[c, w] + rd[c, w])

    def fleg(c, w, kind, blk, to):
        hop[(c, w, 4 + kind)] = go(
            rcopy(blk, blk, fs.at[c - 1, w, kind], fr.at[c - 1, w, kind], to[w])
        )

    def spread(c):
        for w in (0, 1):
            fleg(c, w, 1, fac.at[c - 1, :, z], far)
        for w in (0, 1):
            fleg(c, w, 0, fac.at[c - 1, :, z], ring)

    def forward(c):
        for w in (0, 1):
            hop[(c, w, 5)].wait_recv()
            zz = wrapz(z - 2) if w == 0 else wrapz(z + 2)
            fleg(c, w, 3, fac.at[c - 1, w, zz], far)
            fleg(c, w, 2, fac.at[c - 1, :, zz], ring)

    def gathered(c):
        for w in (0, 1):
            for kind in (0, 2, 3):
                hop[(c, w, 4 + kind)].wait_recv()

    def adam(c, put):
        cols = slice(c * CW, c * CW + CW)
        for w in (0, 1):
            rows = slice(w * 32, w * 32 + 32)
            grad = part[w, rank_rows(0, 0), cols]
            first = decay_first * mom[rows, cols] + (1.0 - decay_first) * grad
            second = decay_second * sec[rows, cols] + (1.0 - decay_second) * grad * grad
            mom[rows, cols] = first
            sec[rows, cols] = second
            put(w, (first / bias_first / (jnp.sqrt(second / bias_second) + adam_eps)).astype(BF16))

    def put_home(w, v):
        home[g, w, z] = v

    def put_fac(c):
        def put(w, v):
            fac[c - 1, w, z] = v

        return put

    begin(1)
    begin(0)
    g_in.append(grad_send(1, 512, 256))
    t_in.append(go(rcopy(bas.at[z], lhs.at[:, :, rows_t], ts.at[1], tr.at[1], (d, t2))))
    middle(1)
    middle(0)
    close(1)
    loads[4].wait()
    loads[5].wait()
    for c in m_in:
        c.wait_recv()
    step0, last0 = gather(lambda zz, h: home.at[:, h, zz], us, ur)
    adam(1, put_fac(1))
    spread(1)
    close(0)
    adam(0, put_home)
    blk = home.at[g, :, z]
    q_in = [go(rcopy(blk, blk, qs.at[j], qr.at[j], group[j])) for j in ORDER]
    forward(1)
    for c in g_in[1]:
        c.wait_recv()
    begin(2)
    t_in[1].wait_recv()
    blk = lhs.at[:, :, rows_u]
    t_in.append(go(rcopy(blk, blk, ts.at[2], tr.at[2], core)))
    gathered(1)

    e_in = {}

    def expand(c):
        for j in ORDER + (0,):
            res = jnp.dot(lhs[index(j, 1)], fac[c - 1].reshape(512, CW), preferred_element_type=F32)
            cols = slice((c - 1) * CW, c * CW)
            if j == 0:
                exr[g, :, cols] = res
            else:
                exs[j, :, cols] = res
                e_in[(c, j)] = go(
                    rcopy(
                        exs.at[j, :, cols],
                        exr.at[g, :, cols],
                        es.at[c - 1, j],
                        er.at[c - 1, j],
                        group[j],
                    )
                )

    for c in t_in:
        if c is not t_in[1]:
            c.wait_recv()
    expand(1)
    middle(2)
    close(2)
    adam(2, put_fac(2))
    spread(2)
    for c in q_in:
        c.wait_recv()
    step0(0)
    forward(2)
    step0(1)
    n_in = []
    for j in ORDER:
        rows = span(index(j, 1) * 8, 8)
        n_in.append(go(rcopy(mom.at[rows], nfr.at[g], ns.at[0, j], nr.at[0, j], group[j])))
        n_in.append(go(rcopy(sec.at[rows], nsr.at[g], ns.at[1, j], nr.at[1, j], group[j])))
    nfr[g] = mom[eight]
    nsr[g] = sec[eight]
    gathered(2)
    expand(2)
    step0(2)
    for c in n_in:
        c.wait_recv()
    for k in range(NG):
        at = min(k * (W // 128), TOP) * 128
        of[:, at : at + W] = nfr[k]
        os_[:, at : at + W] = nsr[k]
    loads[2].wait()
    step0(3)
    last0()
    for k in range(NG):
        at = min(k * (W // 128), TOP) * 128
        res = jnp.dot(lhs[g], home[k].reshape(512, CW), preferred_element_type=F32)
        om[:, at : at + CW] = mas[:, at : at + CW] - step_size * res

    def finish(k):
        cols = pl.ds(pl.multiple_of(start_of(k) + CW, 128), W - CW)
        om[:, cols] = mas[:, cols] - step_size * exr[k]

    finish(g)
    for j in ORDER:
        e_in[(1, j)].wait_recv()
        e_in[(2, j)].wait_recv()
        finish(index(j, -1))
    for c in sends:
        c.wait_send()


def local(activations, out_grad, basis, master, first_moment, second_moment):
    dma = pltpu.SemaphoreType.DMA
    sems = [dma((6,))]
    for shape in (
        (8,),
        (2, 4, 2),
        (2, 8),
        (2, 8),
        (8,),
        (12,),
        (6,),
        (3,),
        (NC, 2, 4),
        (2, 2, 4),
        (8,),
        (2, 4, 2),
        (2, 8),
        (2, 8),
    ):
        sems += [dma(shape), dma(shape)]
    return pl.pallas_call(
        kernel,
        out_shape=(
            jax.ShapeDtypeStruct((128, 5504), F32),
            jax.ShapeDtypeStruct((8, 5504), F32),
            jax.ShapeDtypeStruct((8, 5504), F32),
        ),
        in_specs=[pl.BlockSpec(memory_space=pl.ANY)] * 6,
        out_specs=[pl.BlockSpec(memory_space=pltpu.VMEM)] * 3,
        scratch_shapes=[
            pltpu.VMEM((256, 8192), BF16),
            pltpu.VMEM((NG, 256, W), BF16),
            pltpu.VMEM((NZ, NG, 128, 128), BF16),
            pltpu.VMEM((128, 5504), F32),
            pltpu.VMEM((2, 512, 1024), BF16),
            pltpu.VMEM((2, 256, W), F32),
            pltpu.VMEM((NC, 2, 2, 32, CW), F32),
            pltpu.VMEM((NC, 2, 32, CW), F32),
            pltpu.VMEM((NC, 2, 2, 32, CW), F32),
            pltpu.VMEM((NC, 2, 2, 32, CW), F32),
            pltpu.VMEM((64, W), F32),
            pltpu.VMEM((64, W), F32),
            pltpu.VMEM((NG, 8, W), F32),
            pltpu.VMEM((NG, 8, W), F32),
            pltpu.VMEM((2, 2, NZ, 32, CW), BF16),
            pltpu.VMEM((NG, 2, NZ, 32, CW), BF16),
            pltpu.VMEM((NG, 128, 512), BF16),
            pltpu.VMEM((NG, 128, W - CW), F32),
            pltpu.VMEM((NG, 128, W - CW), F32),
        ]
        + sems,
        compiler_params=pltpu.CompilerParams(
            collective_id=0, has_side_effects=True, vmem_limit_bytes=56 << 20
        ),
    )(activations, out_grad, basis, master, first_moment, second_moment)


def solution(mesh):
    placed = (
        P("dp", None),
        P("dp", "tensor"),
        P("dp", "tensor"),
        P("dp", "tensor"),
        P("dp", "tensor"),
        P("dp", "tensor"),
    )
    return jax.shard_map(
        local,
        mesh=mesh,
        in_specs=placed,
        out_specs=(P("dp", "tensor"), P("dp", "tensor"), P("dp", "tensor")),
        check_vma=False,
    )
```

```python
import math

import jax
import jax.numpy as jnp
from jax import lax
from jax.experimental import pallas as pl
from jax.experimental.pallas import tpu as pltpu
from jax.sharding import PartitionSpec as P

MESH = pl.DeviceIdType.MESH
F32 = jnp.float32
BF16 = jnp.bfloat16

decay_first = 0.9
decay_second = 0.999
bias_first = 1.0 - math.exp(1000.0 * math.log(decay_first))
bias_second = 1.0 - math.exp(1000.0 * math.log(decay_second))
adam_eps = 1e-08
step_size = 0.025

NX, NZ, NG = 4, 8, 8
W = 768
TOP = 5504 // 128 - W // 128
CW = 256
NC = W // CW
ORDER = (6, 2, 5, 7, 4, 1, 3)


def kernel(
    act_h, og_h, bas_h, mas_h, fm_h, sm_h,
    om, of, os_,
    act, og, bas, mas, projt, part, ra, rb, rc, rd, mom, sec, nfr, nsr, fac, home, lhs, exs, exr,
    lsem, bs, br, zs, zr, gs, gr, ms, mr, p1s, p1r, p2s, p2r, cs, cr,
    ts, tr, rs, rr, fs, fr, qs, qr, us, ur, es, er, ns, nr,
):
    d = lax.axis_index("dp")
    t = lax.axis_index("tensor")
    x = lax.rem(d, 4)
    z = lax.rem(d // 4, 8)
    yh = d // 32
    g = yh * 4 + x

    def dev(yy, zz, xx):
        return yy * 32 + zz * 4 + xx

    def wrapz(v):
        return lax.rem(v + 16, 8)

    def member(j, sign):
        yy = lax.rem(yh + j // 4, 2)
        xx = lax.rem(x + sign * (j % 4) + 4, 4)
        return yy, xx

    def index(j, sign):
        yy, xx = member(j, sign)
        return yy * 4 + xx

    def start_of(k):
        return pl.multiple_of(jnp.minimum(k * (W // 128), TOP) * 128, 128)

    def span(first, size):
        return pl.ds(pl.multiple_of(first, size), size)

    def rcopy(src, dst, s, r, to):
        return pltpu.make_async_remote_copy(
            src_ref=src, dst_ref=dst, send_sem=s, recv_sem=r, device_id=to, device_id_type=MESH
        )

    t1 = t + 1 - 2 * lax.rem(t, 2)
    t2 = lax.rem(t + 2, 4)
    ring = ((dev(yh, wrapz(z + 1), x), t), (dev(yh, wrapz(z - 1), x), t))
    far = ((dev(yh, wrapz(z + 2), x), t), (dev(yh, wrapz(z - 2), x), t))
    dy = dev(1 - yh, z, x)
    group = [None]
    for j in range(1, NG):
        yy, xx = member(j, 1)
        group.append((dev(yy, z, xx), t))
    core = (d, t1)
    yside = ((d, t2), (dy, t2), (dy, t))
    partners = group[1:] + [ring[0], ring[1], far[0], far[1], core, (d, t2), (dy, t2)]

    eight = span(g * 8, 8)
    loads = [
        pltpu.make_async_copy(bas_h, bas.at[z, g], lsem.at[3]),
        pltpu.make_async_copy(act_h, act, lsem.at[0]),
        pltpu.make_async_copy(mas_h, mas, lsem.at[1]),
        pltpu.make_async_copy(og_h.at[:, pl.ds(start_of(g), W)], og.at[g], lsem.at[2]),
        pltpu.make_async_copy(fm_h.at[:, pl.ds(start_of(g), W)], mom.at[eight], lsem.at[4]),
        pltpu.make_async_copy(sm_h.at[:, pl.ds(start_of(g), W)], sec.at[eight], lsem.at[5]),
    ]
    for c in loads:
        c.start()

    barrier = pltpu.get_barrier_semaphore()
    for p in partners:
        pl.semaphore_signal(barrier, inc=1, device_id=p, device_id_type=MESH)
    pl.semaphore_wait(barrier, len(partners))

    sends = []

    def go(c):
        c.start()
        sends.append(c)
        return c

    b_in = [go(rcopy(bas_h, bas.at[z, g], bs.at[j], br.at[j], group[j])) for j in ORDER]
    for c in b_in:
        c.wait_recv()
    loads[0].wait()

    def hops(s):
        return [(w, h) for h in (0, 1) for w in (0, 1) if s < 3 or w == h]

    def gather(block, send, recv):
        moving = {}

        def send_step(s):
            for w, h in hops(s):
                if s > 0:
                    moving[(s - 1, w, h)].wait_recv()
                zz = wrapz(z - s) if w == 0 else wrapz(z + s)
                blk = block(zz, h)
                moving[(s, w, h)] = go(rcopy(blk, blk, send.at[w, s, h], recv.at[w, s, h], ring[w]))

        def last():
            for s in (2, 3):
                for w, h in hops(s):
                    if (s, w, h) in moving and not (s == 2 and (w, h) in hops(3)):
                        moving[(s, w, h)].wait_recv()

        return send_step, last

    def project(zz, h):
        return jnp.dot(
            act[:, span((h * 32 + zz * 4) * 128, 512)],
            bas[zz, h * 4 : h * 4 + 4].reshape(512, 128),
            preferred_element_type=F32,
        )

    step, last = gather(lambda zz, h: bas.at[zz, pl.ds(h * 4, 4)], zs, zr)
    step(0)

    def grad_send(i, first, size):
        return [
            go(
                rcopy(
                    og_h.at[:, pl.ds(pl.multiple_of(start_of(index(j, 1)) + first, 128), size)],
                    og.at[g, :, pl.ds(first, size)],
                    gs.at[i, j],
                    gr.at[i, j],
                    group[j],
                )
            )
            for j in ORDER
        ]

    g_in = [grad_send(0, 0, 512)]
    rows_t, rows_u = span(t * 128, 128), span(t2 * 128, 128)
    t_in = [go(rcopy(bas.at[z], lhs.at[:, :, rows_t], ts.at[0], tr.at[0], core))]
    lhs[:, :, rows_t] = bas[z]
    loads[1].wait()
    total = project(z, 0) + project(z, 1)
    for s in range(1, 4):
        step(s)
        for w, h in hops(s - 1):
            if s < 3 or (w, h) in hops(3):
                total = total + project(wrapz(z - s) if w == 0 else wrapz(z + s), h)
    last()
    for w, h in hops(2):
        if (w, h) not in hops(3):
            total = total + project(wrapz(z - 3) if w == 0 else wrapz(z + 3), h)
    for w, h in hops(3):
        total = total + project(wrapz(z - 4), h)

    top_t, low_t = span(t * 128, 64), pl.ds(pl.multiple_of(t * 128 + 64, 64), 64)
    top_u, low_u = span(t2 * 128, 64), pl.ds(pl.multiple_of(t2 * 128 + 64, 64), 64)
    cols_x = span(x * 256, 256)
    projt[yh, rows_t, cols_x] = total.T.astype(BF16)
    blk = projt.at[yh, top_t, cols_x]
    xa = [go(rcopy(blk, blk, p1s.at[j], p1r.at[j], group[j])) for j in (2, 1, 3)]
    blk = projt.at[yh, low_t, cols_x]
    yb = [go(rcopy(blk, blk, p1s.at[4 + i], p1r.at[4 + i], to)) for i, to in enumerate(yside)]
    for c in xa:
        c.wait_recv()
    blk = projt.at[yh, top_t]
    ya = [go(rcopy(blk, blk, p2s.at[i], p2r.at[i], to)) for i, to in enumerate(yside)]
    for c in yb:
        c.wait_recv()
    xb = []
    for i, rows in enumerate((low_t, low_u)):
        blk = projt.at[:, rows, cols_x]
        xb += [go(rcopy(blk, blk, p2s.at[4 * i + 3 + j], p2r.at[4 * i + 3 + j], group[j])) for j in (2, 1, 3)]
    m_in = []
    for j in ORDER:
        cols = pl.ds(start_of(index(j, 1)), W)
        m_in.append(go(rcopy(fm_h.at[:, cols], mom.at[eight], ms.at[0, j], mr.at[0, j], group[j])))
        m_in.append(go(rcopy(sm_h.at[:, cols], sec.at[eight], ms.at[1, j], mr.at[1, j], group[j])))
    blk = projt.at[yh, top_t]
    c_in = [go(rcopy(blk, blk, cs.at[0], cr.at[0], core))]
    for i, (rows, yy) in enumerate([(top_u, yh), (top_u, 1 - yh), (top_t, 1 - yh)]):
        ya[i].wait_recv()
        blk = projt.at[yy, rows]
        c_in.append(go(rcopy(blk, blk, cs.at[i + 1], cr.at[i + 1], core)))
    for i, rows in enumerate((low_t, low_u)):
        for c in xb[3 * i : 3 * i + 3]:
            c.wait_recv()
        blk = projt.at[:, rows]
        c_in.append(go(rcopy(blk, blk, cs.at[i + 4], cr.at[i + 4], core)))
    for c in c_in:
        c.wait_recv()
    loads[3].wait()
    for c in g_in[0]:
        c.wait_recv()

    def multiply(c):
        cols = slice(c * CW, c * CW + CW)
        total = jnp.dot(
            projt[0], og[0:4, :, cols].reshape(1024, CW), preferred_element_type=F32
        ) + jnp.dot(projt[1], og[4:8, :, cols].reshape(1024, CW), preferred_element_type=F32)
        part[:, :, cols] = total.reshape(2, 256, CW)

    def rank_rows(w, away):
        return span(wrapz(z + away if w == 0 else z - away) * 32, 32)

    hop = {}

    def leg(c, w, kind, src, dst, to):
        hop[(c, w, kind)] = go(rcopy(src, dst.at[c, w], rs.at[c, w, kind], rr.at[c, w, kind], to[w]))

    def begin(c):
        multiply(c)
        cols = pl.ds(c * CW, CW)
        for w in (0, 1):
            leg(c, w, 0, part.at[:, rank_rows(w, 3), cols], ra, ring)
            leg(c, w, 1, part.at[w, rank_rows(w, 4), cols], rb, far)
        for w in (0, 1):
            leg(c, w, 2, part.at[:, rank_rows(w, 1), cols], rc, ring)

    def middle(c):
        cols = pl.ds(c * CW, CW)
        for w in (0, 1):
            rows = rank_rows(w, 2)
            hop[(c, w, 0)].wait_recv()
            part[:, rows, cols] = part[:, rows, cols] + ra[c, w]
            hop[(c, w, 1)].wait_recv()
            part[w, rows, cols] = part[w, rows, cols] + rb[c, w]
            leg(c, w, 3, part.at[:, rows, cols], rd, far)

    def close(c):
        cols = pl.ds(c * CW, CW)
        rows = rank_rows(0, 0)
        for w in (0, 1):
            hop[(c, w, 2)].wait_recv()
            hop[(c, w, 3)].wait_recv()
            part[:, rows, cols] = part[:, rows, cols] + (rc[c, w] + rd[c, w])

    def fleg(c, w, kind, blk, to):
        hop[(c, w, 4 + kind)] = go(
            rcopy(blk, blk, fs.at[c - 1, w, kind], fr.at[c - 1, w, kind], to[w])
        )

    def spread(c):
        for w in (0, 1):
            fleg(c, w, 1, fac.at[c - 1, :, z], far)
        for w in (0, 1):
            fleg(c, w, 0, fac.at[c - 1, :, z], ring)

    def forward(c):
        for w in (0, 1):
            hop[(c, w, 5)].wait_recv()
            zz = wrapz(z - 2) if w == 0 else wrapz(z + 2)
            fleg(c, w, 3, fac.at[c - 1, w, zz], far)
            fleg(c, w, 2, fac.at[c - 1, :, zz], ring)

    def gathered(c):
        for w in (0, 1):
            for kind in (0, 2, 3):
                hop[(c, w, 4 + kind)].wait_recv()

    def adam(c, put):
        cols = slice(c * CW, c * CW + CW)
        for w in (0, 1):
            rows = slice(w * 32, w * 32 + 32)
            grad = part[w, rank_rows(0, 0), cols]
            first = decay_first * mom[rows, cols] + (1.0 - decay_first) * grad
            second = decay_second * sec[rows, cols] + (1.0 - decay_second) * grad * grad
            mom[rows, cols] = first
            sec[rows, cols] = second
            put(w, (first / bias_first / (jnp.sqrt(second / bias_second) + adam_eps)).astype(BF16))

    def put_home(w, v):
        home[g, w, z] = v

    def put_fac(c):
        def put(w, v):
            fac[c - 1, w, z] = v

        return put

    begin(1)
    begin(0)
    g_in.append(grad_send(1, 512, 256))
    t_in.append(go(rcopy(bas.at[z], lhs.at[:, :, rows_t], ts.at[1], tr.at[1], (d, t2))))
    middle(1)
    middle(0)
    close(1)
    loads[4].wait()
    loads[5].wait()
    for c in m_in:
        c.wait_recv()
    step0, last0 = gather(lambda zz, h: home.at[:, h, zz], us, ur)
    adam(1, put_fac(1))
    spread(1)
    close(0)
    adam(0, put_home)
    blk = home.at[g, :, z]
    q_in = [go(rcopy(blk, blk, qs.at[j], qr.at[j], group[j])) for j in ORDER]
    forward(1)
    for c in g_in[1]:
        c.wait_recv()
    begin(2)
    t_in[1].wait_recv()
    blk = lhs.at[:, :, rows_u]
    t_in.append(go(rcopy(blk, blk, ts.at[2], tr.at[2], core)))
    gathered(1)

    e_in = {}

    def expand(c):
        for j in ORDER + (0,):
            res = jnp.dot(lhs[index(j, 1)], fac[c - 1].reshape(512, CW), preferred_element_type=F32)
            cols = slice((c - 1) * CW, c * CW)
            if j == 0:
                exr[g, :, cols] = res
            else:
                exs[j, :, cols] = res
                e_in[(c, j)] = go(
                    rcopy(
                        exs.at[j, :, cols],
                        exr.at[g, :, cols],
                        es.at[c - 1, j],
                        er.at[c - 1, j],
                        group[j],
                    )
                )

    for c in t_in:
        if c is not t_in[1]:
            c.wait_recv()
    expand(1)
    middle(2)
    close(2)
    adam(2, put_fac(2))
    spread(2)
    for c in q_in:
        c.wait_recv()
    step0(0)
    forward(2)
    step0(1)
    n_in = []
    for j in ORDER:
        rows = span(index(j, 1) * 8, 8)
        n_in.append(go(rcopy(mom.at[rows], nfr.at[g], ns.at[0, j], nr.at[0, j], group[j])))
        n_in.append(go(rcopy(sec.at[rows], nsr.at[g], ns.at[1, j], nr.at[1, j], group[j])))
    nfr[g] = mom[eight]
    nsr[g] = sec[eight]
    gathered(2)
    expand(2)
    step0(2)
    loads[2].wait()
    step0(3)
    for c in n_in:
        c.wait_recv()
    for k in range(NG):
        at = min(k * (W // 128), TOP) * 128
        of[:, at : at + W] = nfr[k]
        os_[:, at : at + W] = nsr[k]
    last0()
    for k in range(NG):
        at = min(k * (W // 128), TOP) * 128
        res = jnp.dot(lhs[g], home[k].reshape(512, CW), preferred_element_type=F32)
        om[:, at : at + CW] = mas[:, at : at + CW] - step_size * res

    def finish(k):
        cols = pl.ds(pl.multiple_of(start_of(k) + CW, 128), W - CW)
        om[:, cols] = mas[:, cols] - step_size * exr[k]

    finish(g)
    for j in ORDER:
        e_in[(1, j)].wait_recv()
        e_in[(2, j)].wait_recv()
        finish(index(j, -1))
    for c in sends:
        c.wait_send()


PIECES = 8


def write(om_h, of_h, os_h, om, of, os_, big, first, second, sem):
    rows = om_h.shape[0] // PIECES
    cut = [pl.ds(i * rows, rows) for i in range(PIECES)]
    legs = [(om_h.at[c], big.at[c], om.at[c]) for c in cut] + [(of_h, first, of), (os_h, second, os_)]
    loads = [pltpu.make_async_copy(a, b, sem.at[0, i]) for i, (a, b, _) in enumerate(legs)]
    stores = [pltpu.make_async_copy(b, c, sem.at[1, i]) for i, (_, b, c) in enumerate(legs)]
    for c in loads:
        c.start()
    for c, e in zip(loads, stores):
        c.wait()
        e.start()
    for e in stores:
        e.wait()


def local(activations, out_grad, basis, master, first_moment, second_moment):
    dma = pltpu.SemaphoreType.DMA
    sems = [dma((6,))]
    for shape in (
        (8,),
        (2, 4, 2),
        (2, 8),
        (2, 8),
        (8,),
        (12,),
        (6,),
        (3,),
        (NC, 2, 4),
        (2, 2, 4),
        (8,),
        (2, 4, 2),
        (2, 8),
        (2, 8),
    ):
        sems += [dma(shape), dma(shape)]
    results = pl.pallas_call(
        kernel,
        out_shape=(
            jax.ShapeDtypeStruct((128, 5504), F32),
            jax.ShapeDtypeStruct((8, 5504), F32),
            jax.ShapeDtypeStruct((8, 5504), F32),
        ),
        in_specs=[pl.BlockSpec(memory_space=pl.ANY)] * 6,
        out_specs=[pl.BlockSpec(memory_space=pltpu.VMEM)] * 3,
        scratch_shapes=[
            pltpu.VMEM((256, 8192), BF16),
            pltpu.VMEM((NG, 256, W), BF16),
            pltpu.VMEM((NZ, NG, 128, 128), BF16),
            pltpu.VMEM((128, 5504), F32),
            pltpu.VMEM((2, 512, 1024), BF16),
            pltpu.VMEM((2, 256, W), F32),
            pltpu.VMEM((NC, 2, 2, 32, CW), F32),
            pltpu.VMEM((NC, 2, 32, CW), F32),
            pltpu.VMEM((NC, 2, 2, 32, CW), F32),
            pltpu.VMEM((NC, 2, 2, 32, CW), F32),
            pltpu.VMEM((64, W), F32),
            pltpu.VMEM((64, W), F32),
            pltpu.VMEM((NG, 8, W), F32),
            pltpu.VMEM((NG, 8, W), F32),
            pltpu.VMEM((2, 2, NZ, 32, CW), BF16),
            pltpu.VMEM((NG, 2, NZ, 32, CW), BF16),
            pltpu.VMEM((NG, 128, 512), BF16),
            pltpu.VMEM((NG, 128, W - CW), F32),
            pltpu.VMEM((NG, 128, W - CW), F32),
        ]
        + sems,
        compiler_params=pltpu.CompilerParams(
            collective_id=0, has_side_effects=True, vmem_limit_bytes=56 << 20
        ),
    )(activations, out_grad, basis, master, first_moment, second_moment)
    return pl.pallas_call(
        write,
        out_shape=tuple(jax.ShapeDtypeStruct(r.shape, r.dtype) for r in results),
        in_specs=[pl.BlockSpec(memory_space=pl.ANY)] * 3,
        out_specs=[pl.BlockSpec(memory_space=pl.ANY)] * 3,
        scratch_shapes=[pltpu.VMEM(r.shape, r.dtype) for r in results] + [dma((2, PIECES + 2))],
    )(*results)


def solution(mesh):
    placed = (
        P("dp", None),
        P("dp", "tensor"),
        P("dp", "tensor"),
        P("dp", "tensor"),
        P("dp", "tensor"),
        P("dp", "tensor"),
    )
    return jax.shard_map(
        local,
        mesh=mesh,
        in_specs=placed,
        out_specs=(P("dp", "tensor"), P("dp", "tensor"), P("dp", "tensor")),
        check_vma=False,
    )
```

```python
import math

import jax
import jax.numpy as jnp
from jax import lax
from jax.experimental import pallas as pl
from jax.experimental.pallas import tpu as pltpu
from jax.sharding import PartitionSpec as P

MESH = pl.DeviceIdType.MESH
F32 = jnp.float32
BF16 = jnp.bfloat16

decay_first = 0.9
decay_second = 0.999
bias_first = 1.0 - math.exp(1000.0 * math.log(decay_first))
bias_second = 1.0 - math.exp(1000.0 * math.log(decay_second))
adam_eps = 1e-08
step_size = 0.025

NX, NZ, NG = 4, 8, 8
W = 768
TOP = 5504 // 128 - W // 128
CW = 256
NC = W // CW
ORDER = (6, 2, 5, 7, 4, 1, 3)


def kernel(
    act_h, og_h, bas_h, mas_h, fm_h, sm_h,
    om, of, os_,
    act, og, bas, mas, projt, part, ra, rb, rc, rd, mom, sec, nfr, nsr, fac, home, lhs, exs, exr,
    lsem, bs, br, zs, zr, gs, gr, ms, mr, p1s, p1r, p2s, p2r, cs, cr,
    ts, tr, rs, rr, fs, fr, qs, qr, us, ur, es, er, ns, nr,
):
    d = lax.axis_index("dp")
    t = lax.axis_index("tensor")
    x = lax.rem(d, 4)
    z = lax.rem(d // 4, 8)
    yh = d // 32
    g = yh * 4 + x

    def dev(yy, zz, xx):
        return yy * 32 + zz * 4 + xx

    def wrapz(v):
        return lax.rem(v + 16, 8)

    def member(j, sign):
        yy = lax.rem(yh + j // 4, 2)
        xx = lax.rem(x + sign * (j % 4) + 4, 4)
        return yy, xx

    def index(j, sign):
        yy, xx = member(j, sign)
        return yy * 4 + xx

    def start_of(k):
        return pl.multiple_of(jnp.minimum(k * (W // 128), TOP) * 128, 128)

    def span(first, size):
        return pl.ds(pl.multiple_of(first, size), size)

    def rcopy(src, dst, s, r, to):
        return pltpu.make_async_remote_copy(
            src_ref=src, dst_ref=dst, send_sem=s, recv_sem=r, device_id=to, device_id_type=MESH
        )

    t1 = t + 1 - 2 * lax.rem(t, 2)
    t2 = lax.rem(t + 2, 4)
    ring = ((dev(yh, wrapz(z + 1), x), t), (dev(yh, wrapz(z - 1), x), t))
    far = ((dev(yh, wrapz(z + 2), x), t), (dev(yh, wrapz(z - 2), x), t))
    dy = dev(1 - yh, z, x)
    group = [None]
    for j in range(1, NG):
        yy, xx = member(j, 1)
        group.append((dev(yy, z, xx), t))
    core = (d, t1)
    yside = ((d, t2), (dy, t2), (dy, t))
    partners = group[1:] + [ring[0], ring[1], far[0], far[1], core, (d, t2), (dy, t2)]

    eight = span(g * 8, 8)
    loads = [
        pltpu.make_async_copy(bas_h, bas.at[z, g], lsem.at[3]),
        pltpu.make_async_copy(act_h, act, lsem.at[0]),
        pltpu.make_async_copy(mas_h, mas, lsem.at[1]),
        pltpu.make_async_copy(og_h.at[:, pl.ds(start_of(g), W)], og.at[g], lsem.at[2]),
        pltpu.make_async_copy(fm_h.at[:, pl.ds(start_of(g), W)], mom.at[eight], lsem.at[4]),
        pltpu.make_async_copy(sm_h.at[:, pl.ds(start_of(g), W)], sec.at[eight], lsem.at[5]),
    ]
    for c in loads:
        c.start()

    barrier = pltpu.get_barrier_semaphore()
    for p in partners:
        pl.semaphore_signal(barrier, inc=1, device_id=p, device_id_type=MESH)
    pl.semaphore_wait(barrier, len(partners))

    sends = []

    def go(c):
        c.start()
        sends.append(c)
        return c

    b_in = [go(rcopy(bas_h, bas.at[z, g], bs.at[j], br.at[j], group[j])) for j in ORDER]
    for c in b_in:
        c.wait_recv()
    loads[0].wait()

    def hops(s):
        return [(w, h) for h in (0, 1) for w in (0, 1) if s < 3 or w == h]

    def gather(block, send, recv):
        moving = {}

        def send_step(s):
            for w, h in hops(s):
                if s > 0:
                    moving[(s - 1, w, h)].wait_recv()
                zz = wrapz(z - s) if w == 0 else wrapz(z + s)
                blk = block(zz, h)
                moving[(s, w, h)] = go(rcopy(blk, blk, send.at[w, s, h], recv.at[w, s, h], ring[w]))

        def last():
            for s in (2, 3):
                for w, h in hops(s):
                    if (s, w, h) in moving and not (s == 2 and (w, h) in hops(3)):
                        moving[(s, w, h)].wait_recv()

        return send_step, last

    def project(zz, h):
        return jnp.dot(
            act[:, span((h * 32 + zz * 4) * 128, 512)],
            bas[zz, h * 4 : h * 4 + 4].reshape(512, 128),
            preferred_element_type=F32,
        )

    step, last = gather(lambda zz, h: bas.at[zz, pl.ds(h * 4, 4)], zs, zr)
    step(0)

    def grad_send(i, first, size):
        return [
            go(
                rcopy(
                    og_h.at[:, pl.ds(pl.multiple_of(start_of(index(j, 1)) + first, 128), size)],
                    og.at[g, :, pl.ds(first, size)],
                    gs.at[i, j],
                    gr.at[i, j],
                    group[j],
                )
            )
            for j in ORDER
        ]

    g_in = [grad_send(0, 0, 512)]
    rows_t, rows_u = span(t * 128, 128), span(t2 * 128, 128)
    t_in = [go(rcopy(bas.at[z], lhs.at[:, :, rows_t], ts.at[0], tr.at[0], core))]
    lhs[:, :, rows_t] = bas[z]
    loads[1].wait()
    total = project(z, 0) + project(z, 1)
    for s in range(1, 4):
        step(s)
        for w, h in hops(s - 1):
            if s < 3 or (w, h) in hops(3):
                total = total + project(wrapz(z - s) if w == 0 else wrapz(z + s), h)
    last()
    for w, h in hops(2):
        if (w, h) not in hops(3):
            total = total + project(wrapz(z - 3) if w == 0 else wrapz(z + 3), h)
    for w, h in hops(3):
        total = total + project(wrapz(z - 4), h)

    top_t, low_t = span(t * 128, 64), pl.ds(pl.multiple_of(t * 128 + 64, 64), 64)
    top_u, low_u = span(t2 * 128, 64), pl.ds(pl.multiple_of(t2 * 128 + 64, 64), 64)
    cols_x = span(x * 256, 256)
    projt[yh, rows_t, cols_x] = total.T.astype(BF16)
    blk = projt.at[yh, top_t, cols_x]
    xa = [go(rcopy(blk, blk, p1s.at[j], p1r.at[j], group[j])) for j in (2, 1, 3)]
    blk = projt.at[yh, low_t, cols_x]
    yb = [go(rcopy(blk, blk, p1s.at[4 + i], p1r.at[4 + i], to)) for i, to in enumerate(yside)]
    for c in xa:
        c.wait_recv()
    blk = projt.at[yh, top_t]
    ya = [go(rcopy(blk, blk, p2s.at[i], p2r.at[i], to)) for i, to in enumerate(yside)]
    for c in yb:
        c.wait_recv()
    xb = []
    for i, rows in enumerate((low_t, low_u)):
        blk = projt.at[:, rows, cols_x]
        xb += [go(rcopy(blk, blk, p2s.at[4 * i + 3 + j], p2r.at[4 * i + 3 + j], group[j])) for j in (2, 1, 3)]
    m_in = []
    for j in ORDER:
        cols = pl.ds(start_of(index(j, 1)), W)
        m_in.append(go(rcopy(fm_h.at[:, cols], mom.at[eight], ms.at[0, j], mr.at[0, j], group[j])))
        m_in.append(go(rcopy(sm_h.at[:, cols], sec.at[eight], ms.at[1, j], mr.at[1, j], group[j])))
    blk = projt.at[yh, top_t]
    c_in = [go(rcopy(blk, blk, cs.at[0], cr.at[0], core))]
    for i, (rows, yy) in enumerate([(top_u, yh), (top_u, 1 - yh), (top_t, 1 - yh)]):
        ya[i].wait_recv()
        blk = projt.at[yy, rows]
        c_in.append(go(rcopy(blk, blk, cs.at[i + 1], cr.at[i + 1], core)))
    for i, rows in enumerate((low_t, low_u)):
        for c in xb[3 * i : 3 * i + 3]:
            c.wait_recv()
        blk = projt.at[:, rows]
        c_in.append(go(rcopy(blk, blk, cs.at[i + 4], cr.at[i + 4], core)))
    for c in c_in:
        c.wait_recv()
    loads[3].wait()
    for c in g_in[0]:
        c.wait_recv()

    def multiply(c):
        cols = slice(c * CW, c * CW + CW)
        total = jnp.dot(
            projt[0], og[0:4, :, cols].reshape(1024, CW), preferred_element_type=F32
        ) + jnp.dot(projt[1], og[4:8, :, cols].reshape(1024, CW), preferred_element_type=F32)
        part[:, :, cols] = total.reshape(2, 256, CW)

    def rank_rows(w, away):
        return span(wrapz(z + away if w == 0 else z - away) * 32, 32)

    hop = {}

    def leg(c, w, kind, src, dst, to):
        hop[(c, w, kind)] = go(rcopy(src, dst.at[c, w], rs.at[c, w, kind], rr.at[c, w, kind], to[w]))

    def begin(c):
        multiply(c)
        cols = pl.ds(c * CW, CW)
        for w in (0, 1):
            leg(c, w, 0, part.at[:, rank_rows(w, 3), cols], ra, ring)
            leg(c, w, 1, part.at[w, rank_rows(w, 4), cols], rb, far)
        for w in (0, 1):
            leg(c, w, 2, part.at[:, rank_rows(w, 1), cols], rc, ring)

    def middle(c):
        cols = pl.ds(c * CW, CW)
        for w in (0, 1):
            rows = rank_rows(w, 2)
            hop[(c, w, 0)].wait_recv()
            part[:, rows, cols] = part[:, rows, cols] + ra[c, w]
            hop[(c, w, 1)].wait_recv()
            part[w, rows, cols] = part[w, rows, cols] + rb[c, w]
            leg(c, w, 3, part.at[:, rows, cols], rd, far)

    def close(c):
        cols = pl.ds(c * CW, CW)
        rows = rank_rows(0, 0)
        for w in (0, 1):
            hop[(c, w, 2)].wait_recv()
            hop[(c, w, 3)].wait_recv()
            part[:, rows, cols] = part[:, rows, cols] + (rc[c, w] + rd[c, w])

    def fleg(c, w, kind, blk, to):
        hop[(c, w, 4 + kind)] = go(
            rcopy(blk, blk, fs.at[c - 1, w, kind], fr.at[c - 1, w, kind], to[w])
        )

    def spread(c):
        for w in (0, 1):
            fleg(c, w, 1, fac.at[c - 1, :, z], far)
        for w in (0, 1):
            fleg(c, w, 0, fac.at[c - 1, :, z], ring)

    def forward(c):
        for w in (0, 1):
            hop[(c, w, 5)].wait_recv()
            zz = wrapz(z - 2) if w == 0 else wrapz(z + 2)
            fleg(c, w, 3, fac.at[c - 1, w, zz], far)
            fleg(c, w, 2, fac.at[c - 1, :, zz], ring)

    def gathered(c):
        for w in (0, 1):
            for kind in (0, 2, 3):
                hop[(c, w, 4 + kind)].wait_recv()

    def adam(c, put):
        cols = slice(c * CW, c * CW + CW)
        for w in (0, 1):
            rows = slice(w * 32, w * 32 + 32)
            grad = part[w, rank_rows(0, 0), cols]
            first = decay_first * mom[rows, cols] + (1.0 - decay_first) * grad
            second = decay_second * sec[rows, cols] + (1.0 - decay_second) * grad * grad
            mom[rows, cols] = first
            sec[rows, cols] = second
            put(w, (first / bias_first / (jnp.sqrt(second / bias_second) + adam_eps)).astype(BF16))

    def put_home(w, v):
        home[g, w, z] = v

    def put_fac(c):
        def put(w, v):
            fac[c - 1, w, z] = v

        return put

    begin(1)
    begin(0)
    g_in.append(grad_send(1, 512, 256))
    t_in.append(go(rcopy(bas.at[z], lhs.at[:, :, rows_t], ts.at[1], tr.at[1], (d, t2))))
    middle(1)
    middle(0)
    close(1)
    loads[4].wait()
    loads[5].wait()
    for c in m_in:
        c.wait_recv()
    step0, last0 = gather(lambda zz, h: home.at[:, h, zz], us, ur)
    adam(1, put_fac(1))
    spread(1)
    close(0)
    adam(0, put_home)
    blk = home.at[g, :, z]
    q_in = [go(rcopy(blk, blk, qs.at[j], qr.at[j], group[j])) for j in ORDER]
    forward(1)
    for c in g_in[1]:
        c.wait_recv()
    begin(2)
    t_in[1].wait_recv()
    blk = lhs.at[:, :, rows_u]
    t_in.append(go(rcopy(blk, blk, ts.at[2], tr.at[2], core)))
    gathered(1)

    e_in = {}

    def expand(c):
        for j in ORDER + (0,):
            res = jnp.dot(lhs[index(j, 1)], fac[c - 1].reshape(512, CW), preferred_element_type=F32)
            cols = slice((c - 1) * CW, c * CW)
            if j == 0:
                exr[g, :, cols] = res
            else:
                exs[j, :, cols] = res
                e_in[(c, j)] = go(
                    rcopy(
                        exs.at[j, :, cols],
                        exr.at[g, :, cols],
                        es.at[c - 1, j],
                        er.at[c - 1, j],
                        group[j],
                    )
                )

    for c in t_in:
        if c is not t_in[1]:
            c.wait_recv()
    middle(2)
    expand(1)
    close(2)
    adam(2, put_fac(2))
    spread(2)
    n_in = []
    for j in ORDER:
        rows = span(index(j, 1) * 8, 8)
        n_in.append(go(rcopy(mom.at[rows], nfr.at[g], ns.at[0, j], nr.at[0, j], group[j])))
        n_in.append(go(rcopy(sec.at[rows], nsr.at[g], ns.at[1, j], nr.at[1, j], group[j])))
    nfr[g] = mom[eight]
    nsr[g] = sec[eight]
    for c in q_in:
        c.wait_recv()
    step0(0)
    forward(2)
    step0(1)
    gathered(2)
    expand(2)
    step0(2)
    loads[2].wait()
    step0(3)
    for c in n_in:
        c.wait_recv()
    for k in range(NG):
        at = min(k * (W // 128), TOP) * 128
        of[:, at : at + W] = nfr[k]
        os_[:, at : at + W] = nsr[k]
    last0()
    for k in range(NG):
        at = min(k * (W // 128), TOP) * 128
        res = jnp.dot(lhs[g], home[k].reshape(512, CW), preferred_element_type=F32)
        om[:, at : at + CW] = mas[:, at : at + CW] - step_size * res

    def finish(k):
        cols = pl.ds(pl.multiple_of(start_of(k) + CW, 128), W - CW)
        om[:, cols] = mas[:, cols] - step_size * exr[k]

    finish(g)
    for j in ORDER:
        e_in[(1, j)].wait_recv()
        e_in[(2, j)].wait_recv()
        finish(index(j, -1))
    for c in sends:
        c.wait_send()


PIECES = 8


def write(om_h, of_h, os_h, om, of, os_, big, first, second, sem):
    rows = om_h.shape[0] // PIECES
    cut = [pl.ds(i * rows, rows) for i in range(PIECES)]
    legs = [(om_h.at[c], big.at[c], om.at[c]) for c in cut] + [(of_h, first, of), (os_h, second, os_)]
    loads = [pltpu.make_async_copy(a, b, sem.at[0, i]) for i, (a, b, _) in enumerate(legs)]
    stores = [pltpu.make_async_copy(b, c, sem.at[1, i]) for i, (_, b, c) in enumerate(legs)]
    for c in loads:
        c.start()
    for c, e in zip(loads, stores):
        c.wait()
        e.start()
    for e in stores:
        e.wait()


def local(activations, out_grad, basis, master, first_moment, second_moment):
    dma = pltpu.SemaphoreType.DMA
    sems = [dma((6,))]
    for shape in (
        (8,),
        (2, 4, 2),
        (2, 8),
        (2, 8),
        (8,),
        (12,),
        (6,),
        (3,),
        (NC, 2, 4),
        (2, 2, 4),
        (8,),
        (2, 4, 2),
        (2, 8),
        (2, 8),
    ):
        sems += [dma(shape), dma(shape)]
    results = pl.pallas_call(
        kernel,
        out_shape=(
            jax.ShapeDtypeStruct((128, 5504), F32),
            jax.ShapeDtypeStruct((8, 5504), F32),
            jax.ShapeDtypeStruct((8, 5504), F32),
        ),
        in_specs=[pl.BlockSpec(memory_space=pl.ANY)] * 6,
        out_specs=[pl.BlockSpec(memory_space=pltpu.VMEM)] * 3,
        scratch_shapes=[
            pltpu.VMEM((256, 8192), BF16),
            pltpu.VMEM((NG, 256, W), BF16),
            pltpu.VMEM((NZ, NG, 128, 128), BF16),
            pltpu.VMEM((128, 5504), F32),
            pltpu.VMEM((2, 512, 1024), BF16),
            pltpu.VMEM((2, 256, W), F32),
            pltpu.VMEM((NC, 2, 2, 32, CW), F32),
            pltpu.VMEM((NC, 2, 32, CW), F32),
            pltpu.VMEM((NC, 2, 2, 32, CW), F32),
            pltpu.VMEM((NC, 2, 2, 32, CW), F32),
            pltpu.VMEM((64, W), F32),
            pltpu.VMEM((64, W), F32),
            pltpu.VMEM((NG, 8, W), F32),
            pltpu.VMEM((NG, 8, W), F32),
            pltpu.VMEM((2, 2, NZ, 32, CW), BF16),
            pltpu.VMEM((NG, 2, NZ, 32, CW), BF16),
            pltpu.VMEM((NG, 128, 512), BF16),
            pltpu.VMEM((NG, 128, W - CW), F32),
            pltpu.VMEM((NG, 128, W - CW), F32),
        ]
        + sems,
        compiler_params=pltpu.CompilerParams(
            collective_id=0, has_side_effects=True, vmem_limit_bytes=56 << 20
        ),
    )(activations, out_grad, basis, master, first_moment, second_moment)
    return pl.pallas_call(
        write,
        out_shape=tuple(jax.ShapeDtypeStruct(r.shape, r.dtype) for r in results),
        in_specs=[pl.BlockSpec(memory_space=pl.ANY)] * 3,
        out_specs=[pl.BlockSpec(memory_space=pl.ANY)] * 3,
        scratch_shapes=[pltpu.VMEM(r.shape, r.dtype) for r in results] + [dma((2, PIECES + 2))],
    )(*results)


def solution(mesh):
    placed = (
        P("dp", None),
        P("dp", "tensor"),
        P("dp", "tensor"),
        P("dp", "tensor"),
        P("dp", "tensor"),
        P("dp", "tensor"),
    )
    return jax.shard_map(
        local,
        mesh=mesh,
        in_specs=placed,
        out_specs=(P("dp", "tensor"), P("dp", "tensor"), P("dp", "tensor")),
        check_vma=False,
    )
```
